32 devices in a mesh: ka: 4 (over y, x), band: 8 (over z, core).
Axes of the slice: x: 2, y: 2, z: 4, core: 2. Of those that a mesh axis runs over, the one named last changes fastest.
Arguments:
- targets: bfloat16 [4, 8, 24, 24, 128], P('ka', 'band'), may hold values from -6 to 6
- occupied: bfloat16 [4, 16, 24, 24, 128], P('ka', 'band'), may hold values from -6 to 6
- wavevectors: int32 [4, 3], replicated, may hold values from 0 to 3
- umklapp: int32 [4, 2, 3], P('ka'), may hold values from -1 to 1
- owners: int32 [4, 2, 2], P('ka'), may hold values from 0 to 7
Outputs:
- exchange: bfloat16 [4, 8, 24, 24, 128], P('ka', 'band')
The draws below stay inside these ranges and needn't reach their ends.
All inputs are finite; a program needn't handle non-finite values.
Results may differ from the reference program's by a relative error of at most 0.017.
Values may be sent and summed in bfloat16 or wider, within the bound.
A program may use at most 64 MiB of HBM per device.

```python
import math
import jax
import jax.numpy as jnp
from jax import lax

NX = 64
NY = 24
NZ = 24
OCC_DEV = 2
STEPS = 2
KGRID = 4
KPTS = 4
BANDS = 8
OCC_BANDS = 16
N_BAND = 8


def place_ends(values, stream_key, smallest, largest):
    longest = values.shape.index(max(values.shape))
    spots = []
    for shift in (0, 1):
        where = [jax.random.randint(jax.random.fold_in(stream_key, axis), (), 0, length) for axis, length in enumerate(values.shape)]
        where[longest] = (where[longest] + shift) % values.shape[longest]
        spots.append(tuple(where))
    return values.at[spots[0]].set(smallest).at[spots[1]].set(largest)


def steps_of(own_key, dims, cuts, least, top_value):
    def one(position, parts):
        heights = jax.random.uniform(jax.random.fold_in(jax.random.fold_in(own_key, 6), position), (parts,), jnp.float32, least / len(cuts), top_value / len(cuts))
        return jnp.repeat(jnp.exp(heights), dims[position] // parts).reshape((-1,) + (1,) * (len(dims) - position - 1))

    factor_of = one(*cuts[0])
    for cut in cuts[1:]:
        factor_of = factor_of * one(*cut)
    return factor_of


def normal_values(stream_key, dims, width, limit, cuts=(), kind=jnp.bfloat16):
    loudness = steps_of(stream_key, dims, cuts, -0.22, 0.18) if cuts else 1.0
    values = jax.random.normal(stream_key, dims, jnp.float32) * width * loudness
    return jnp.minimum(jnp.maximum(values, -limit), limit).astype(kind)


def setup_inputs(seed: int = 0) -> dict:
    splits = jax.random.split(jax.random.key(seed), 6)
    targets = normal_values(splits[0], (KPTS, BANDS, NY, NZ, 2 * NX), 1.0, 6.0, ((0, 4), (1, 8)))
    occupied = normal_values(splits[1], (KPTS, OCC_BANDS, NY, NZ, 2 * NX), 1.0, 6.0, ((0, 4), (1, 8)))
    wavevectors = place_ends(jax.random.randint(splits[2], (KPTS, 3), 0, KGRID), jax.random.fold_in(splits[2], 1), 0, KGRID - 1).astype(jnp.int32)
    umklapp = place_ends(jax.random.randint(splits[3], (KPTS, STEPS, 3), -1, 2), jax.random.fold_in(splits[3], 1), -1, 1).astype(jnp.int32)
    owners = place_ends(jax.random.randint(splits[4], (KPTS, STEPS, OCC_DEV), 0, N_BAND), jax.random.fold_in(splits[4], 1), 0, N_BAND - 1).astype(jnp.int32)
    return dict(targets=targets, occupied=occupied, wavevectors=wavevectors, umklapp=umklapp, owners=owners)


screening_sq = 0.16
spacing = 0.25
prefactor = -0.5


def tables(length):
    indices = jnp.arange(length, dtype=jnp.int32)
    products = (indices[:, None] * indices[None, :]) % length
    angles = products.astype(jnp.float32) * (2.0 * math.pi / length)
    return jnp.cos(angles), jnp.sin(angles)


def last_matrix(length, sign_value):
    cosine, sine_table = tables(length)
    upper_rows = jnp.concatenate([cosine, -sign_value * sine_table], axis=1)
    bottom = jnp.concatenate([sign_value * sine_table, cosine], axis=1)
    return jnp.concatenate([upper_rows, bottom], axis=0).astype(jnp.bfloat16)


def stacked_table(length):
    cosine, sine_table = tables(length)
    return jnp.concatenate([cosine, sine_table], axis=0).astype(jnp.bfloat16)


def along_axis(grid_values, spec, length, sign_value, axis_pos):
    both = jnp.einsum(spec, stacked_table(length).astype(jnp.float32), grid_values.astype(jnp.float32), precision=lax.Precision.HIGHEST)
    cos_part = lax.slice_in_dim(both, 0, length, axis=axis_pos)
    sin_part = lax.slice_in_dim(both, length, 2 * length, axis=axis_pos)
    half_width = both.shape[-1] // 2
    swapped = jnp.concatenate([sin_part[..., half_width:], sin_part[..., :half_width]], axis=-1)
    half_sign = jnp.concatenate([jnp.ones((half_width,), jnp.float32), -jnp.ones((half_width,), jnp.float32)])
    return (cos_part + sign_value * half_sign * swapped).astype(jnp.bfloat16)


def fourier(grid_values, sign_value):
    last_width = grid_values.shape[-1]
    flattened = grid_values.reshape(-1, last_width)
    moved = jnp.dot(flattened.astype(jnp.float32), last_matrix(last_width // 2, sign_value).astype(jnp.float32), precision=lax.Precision.HIGHEST)
    grid_values = moved.astype(jnp.bfloat16).reshape(grid_values.shape)
    grid_values = along_axis(grid_values, "vy,byzc->bvzc", grid_values.shape[1], sign_value, 1)
    grid_values = along_axis(grid_values, "vz,byzc->byvc", grid_values.shape[2], sign_value, 2)
    return grid_values


def coulomb(shift_vec, grid_x, grid_y, grid_z):
    squares = []
    for axis_pos, length in ((0, grid_x), (1, grid_y), (2, grid_z)):
        indices = jnp.arange(length, dtype=jnp.int32)
        signed = jnp.where(indices * 2 < length, indices, indices - length)
        wavenumber = (2.0 * math.pi / (length * spacing)) * (signed.astype(jnp.float32) + shift_vec[axis_pos])
        squares.append(wavenumber * wavenumber)
    square_x = jnp.concatenate([squares[0], squares[0]])
    total_sq = squares[1][:, None, None] + squares[2][None, :, None] + square_x[None, None, :] + screening_sq
    return 4.0 * math.pi / total_sq


def pair_density(visitor, resident):
    half_width = visitor.shape[-1] // 2
    visit_re = visitor[..., :half_width].astype(jnp.float32)
    visit_im = visitor[..., half_width:].astype(jnp.float32)
    res_re = resident[..., :half_width].astype(jnp.float32)
    res_im = resident[..., half_width:].astype(jnp.float32)
    real_part = visit_re * res_re + visit_im * res_im
    imag_part = visit_re * res_im - visit_im * res_re
    return jnp.concatenate([real_part, imag_part], axis=-1).astype(jnp.bfloat16)


def apply_potential(visitor, potential):
    half_width = visitor.shape[-1] // 2
    visit_re = visitor[..., :half_width].astype(jnp.float32)
    visit_im = visitor[..., half_width:].astype(jnp.float32)
    pot_re = potential[..., :half_width].astype(jnp.float32)
    pot_im = potential[..., half_width:].astype(jnp.float32)
    real_part = visit_re * pot_re - visit_im * pot_im
    imag_part = visit_re * pot_im + visit_im * pot_re
    return jnp.concatenate([real_part, imag_part], axis=-1)


def exchange_term(visitor, resident, kernel, cells):
    density = pair_density(visitor, resident)
    spectrum = fourier(density, 1.0)
    screened = (spectrum.astype(jnp.float32) * kernel * (1.0 / cells)).astype(jnp.bfloat16)
    potential = fourier(screened, -1.0)
    return apply_potential(visitor, potential)


def reference(targets, occupied, wavevectors, umklapp, owners):
    k_total = targets.shape[0]
    grid_y, grid_z, last_width = targets.shape[2], targets.shape[3], targets.shape[4]
    grid_x = last_width // 2
    cells = float(grid_x * grid_y * grid_z)

    def one_point(point_index):
        resident = lax.dynamic_index_in_dim(targets, point_index, 0, keepdims=False)
        own_coords = lax.dynamic_index_in_dim(wavevectors, point_index, 0, keepdims=False)
        shifts = lax.dynamic_index_in_dim(umklapp, point_index, 0, keepdims=False)
        choosers = lax.dynamic_index_in_dim(owners, point_index, 0, keepdims=False)
        accumulated = jnp.zeros(resident.shape, jnp.float32)
        for section_index in range(1, STEPS + 1):
            visit_index = ((point_index - section_index) % k_total).astype(jnp.int32)
            visiting = lax.dynamic_index_in_dim(occupied, visit_index, 0, keepdims=False)
            visit_coords = lax.dynamic_index_in_dim(wavevectors, visit_index, 0, keepdims=False)
            shift_vec = (own_coords - visit_coords).astype(jnp.float32) / KGRID + shifts[section_index - 1].astype(jnp.float32)
            kernel = coulomb(shift_vec, grid_x, grid_y, grid_z)
            for slot_index in range(OCC_DEV):
                chosen = (choosers[section_index - 1, slot_index] * OCC_DEV + slot_index).astype(jnp.int32)
                visitor = lax.dynamic_index_in_dim(visiting, chosen, 0, keepdims=False)
                accumulated = accumulated + exchange_term(visitor, resident, kernel, cells)
        return (prefactor * accumulated).astype(jnp.bfloat16)

    return lax.map(one_point, jnp.arange(k_total, dtype=jnp.int32))
```

```python
import functools
import math

import jax
import jax.numpy as jnp
import ml_dtypes
import numpy as np
from jax import lax
from jax.experimental import pallas as pl
from jax.experimental.pallas import tpu as pltpu
from jax.sharding import PartitionSpec as P

OCC_DEV = 2
STEPS = 2
KGRID = 4

screening_sq = 0.16
spacing = 0.25
prefactor = -0.5

MESH = pl.DeviceIdType.MESH
CORES = 2


def tables(length):
    indices = np.arange(length)
    angles = (indices[:, None] * indices[None, :] % length) * (2.0 * math.pi / length)

    def rounded(values):
        return values.astype(np.float32).astype(ml_dtypes.bfloat16).astype(np.float32)

    return rounded(np.cos(angles)), rounded(np.sin(angles))


def x_matrices(length, sign_value):
    cosine, sine = tables(length)
    upper = np.concatenate([cosine, -sign_value * sine], axis=1)
    lower = np.concatenate([sign_value * sine, cosine], axis=1)
    plain = np.concatenate([upper, lower], axis=0)
    turned = np.concatenate(
        [sign_value * plain[:, length:], -sign_value * plain[:, :length]], axis=1
    )
    two = np.eye(OCC_DEV, dtype=np.float32)
    return np.stack([np.kron(two, plain), np.kron(two, turned)])


def yz_matrix(grid_y, grid_z):
    cos_y, sin_y = tables(grid_y)
    cos_z, sin_z = tables(grid_z)
    cosine = np.kron(cos_y, cos_z) - np.kron(sin_y, sin_z)
    sine = np.kron(sin_y, cos_z) + np.kron(cos_y, sin_z)
    return np.concatenate([cosine, sine], axis=1)


def slices_of(cells_yz, devices):
    rows = -(-cells_yz // (devices * 16)) * 16
    return rows, -(-cells_yz // rows)


def visit_kernel(k_total, devices, owners_ref, occ_ref, vis_ref, gath, stage, own_out, own_in,
                 send1, recv1, send_own, recv_own, send2, recv2, send3, recv3):
    point = lax.axis_index("ka")
    me = lax.axis_index("band")
    level, core = lax.div(me, CORES), lax.rem(me, CORES)
    levels = devices // CORES
    cells_yz = occ_ref.shape[1]
    rows, count = slices_of(cells_yz, devices)
    overlap = count * rows - cells_yz

    def start_of(device):
        part = lax.rem(device, count)
        return pl.multiple_of(part * rows - lax.div(part, max(count - 1, 1)) * overlap, 16)

    def point_at(distance):
        return lax.rem(point + distance + k_total, k_total)

    def band_at(distance):
        return lax.rem(me + distance + devices, devices)

    def level_at(distance):
        return lax.rem(level + distance + levels, levels)

    barrier = pltpu.get_barrier_semaphore()
    greeted = [(point, band_at(-d)) for d in range(1, devices)]
    for s in range(1, STEPS + 1):
        greeted += [(point_at(-s), level_at(-d) * CORES + core) for d in range(levels)]
        greeted.append((point_at(s), me))
    for device in greeted:
        pl.semaphore_signal(barrier, inc=1, device_id=device, device_id_type=MESH)
    for s in range(STEPS):
        for r in range(OCC_DEV):
            own_out[s, r] = jnp.full((8, 128), owners_ref[0, s, r], jnp.int32).astype(jnp.float32)
    pl.semaphore_wait(barrier, len(greeted))

    owns = []
    for s in range(1, STEPS + 1):
        copy = pltpu.make_async_remote_copy(
            src_ref=own_out.at[s - 1], dst_ref=own_in.at[s - 1],
            send_sem=send_own.at[s - 1], recv_sem=recv_own.at[s - 1],
            device_id=(point_at(-s), me), device_id_type=MESH)
        copy.start()
        owns.append(copy)
    first = []
    for d in range(1, devices):
        target = band_at(d)
        copy = pltpu.make_async_remote_copy(
            src_ref=occ_ref.at[:, pl.ds(start_of(target), rows), :], dst_ref=gath.at[d],
            send_sem=send1.at[d], recv_sem=recv1.at[d],
            device_id=(point, target), device_id_type=MESH)
        copy.start()
        first.append(copy)
    gath[0] = occ_ref[:, pl.ds(start_of(me), rows), :]
    for copy in owns + first:
        copy.wait_recv()

    second, third = [], []

    def place(device):
        return pl.ds(pl.multiple_of(device * rows, 16), rows)

    for s in range(STEPS):
        for r in range(OCC_DEV):
            owner = own_in[s, r]
            chosen = jnp.zeros((rows // 8, 8, 128), jnp.float32)
            for d in range(devices):
                here = (owner == band_at(-d).astype(jnp.float32))[None]
                chosen = jnp.where(
                    here, gath[d, r].astype(jnp.float32).reshape(rows // 8, 8, 128), chosen
                )
            stage[s, r] = chosen.reshape(rows, 128).astype(jnp.bfloat16)
        for d in range(levels):
            copy = pltpu.make_async_remote_copy(
                src_ref=stage.at[s], dst_ref=vis_ref.at[s, :, place(me), :],
                send_sem=send2.at[s, d], recv_sem=recv2.at[s, d],
                device_id=(point_at(s + 1), level_at(d) * CORES + core), device_id_type=MESH)
            copy.start()
            second.append((s, d, copy))
    for s, d, copy in second:
        source = level_at(-d) * CORES + core
        arrived = vis_ref.at[s, :, place(source), :]
        copy.wait_recv()
        across = pltpu.make_async_remote_copy(
            src_ref=arrived, dst_ref=arrived,
            send_sem=send3.at[s, d], recv_sem=recv3.at[s, d],
            device_id=(point, level * CORES + 1 - core), device_id_type=MESH)
        across.start()
        third.append((s, d, across))
    for _, _, copy in third:
        copy.wait_recv()
    for copy in owns + first:
        copy.wait_send()
    for _, _, copy in second + third:
        copy.wait_send()


def visitors(owners, occupied, k_total, devices):
    cells_yz = occupied.shape[1]
    rows, _ = slices_of(cells_yz, devices)
    levels = devices // CORES
    dma = pltpu.SemaphoreType.DMA
    return pl.pallas_call(
        functools.partial(visit_kernel, k_total, devices),
        out_shape=jax.ShapeDtypeStruct((STEPS, OCC_DEV, devices * rows, 128), jnp.bfloat16),
        in_specs=[pl.BlockSpec(memory_space=pltpu.SMEM), pl.BlockSpec(memory_space=pltpu.VMEM)],
        out_specs=pl.BlockSpec(memory_space=pltpu.VMEM),
        scratch_shapes=[
            pltpu.VMEM((devices, OCC_DEV, rows, 128), jnp.bfloat16),
            pltpu.VMEM((STEPS, OCC_DEV, rows, 128), jnp.bfloat16),
            pltpu.VMEM((STEPS, OCC_DEV, 8, 128), jnp.float32),
            pltpu.VMEM((STEPS, OCC_DEV, 8, 128), jnp.float32),
            dma((devices,)), dma((devices,)), dma((STEPS,)), dma((STEPS,)),
            dma((STEPS, levels)), dma((STEPS, levels)),
            dma((STEPS, levels)), dma((STEPS, levels)),
        ],
        compiler_params=pltpu.CompilerParams(
            collective_id=0, has_side_effects=True, vmem_limit_bytes=32 * 1024 * 1024
        ),
    )(owners, occupied)


def exchange_kernel(k_total, devices, grid, waves_ref, umk_ref, t_ref, vis_ref, w_ref, fwd_ref,
                    inv_ref, out_ref, held):
    grid_y, grid_z, grid_x = grid
    cells_yz = grid_y * grid_z
    cells = float(cells_yz * grid_x)
    rows, _ = slices_of(cells_yz, devices)
    whole = cells_yz // rows * rows
    tail = cells_yz - whole
    point = lax.axis_index("ka")
    width = 2 * grid_x
    lane = lax.broadcasted_iota(jnp.int32, (cells_yz, width), 1)
    low = lane < grid_x

    def swap(values):
        return pltpu.roll(values, grid_x, axis=1)

    def square(dim, length, shift):
        shape = (grid_y, grid_z, width)
        index = lax.broadcasted_iota(jnp.int32, shape, dim)
        if dim == 2:
            index = jnp.where(index < grid_x, index, index - grid_x)
        signed = jnp.where(index * 2 < length, index, index - length)
        wave = 2.0 * math.pi / (length * spacing) * (signed.astype(jnp.float32) + shift)
        return wave * wave

    resident = t_ref[...].astype(jnp.float32)
    swapped = swap(resident)
    total = None
    for s in range(STEPS):
        visit = lax.rem(point - (s + 1) + k_total, k_total)
        shift = [
            (waves_ref[point, a] - waves_ref[visit, a]).astype(jnp.float32) / KGRID
            + umk_ref[0, s, a].astype(jnp.float32)
            for a in range(3)
        ]
        squares = (
            square(0, grid_y, shift[1])
            + square(1, grid_z, shift[2])
            + square(2, grid_x, shift[0])
            + screening_sq
        )
        kernel = (4.0 * math.pi / cells / squares).reshape(cells_yz, width)
        re, im, density = [], [], []
        for r in range(OCC_DEV):
            field = vis_ref[s, r, :whole]
            if tail:
                end = whole + rows
                field = jnp.concatenate([field, vis_ref[s, r, end - tail : end]], axis=0)
            field = field.astype(jnp.float32)
            other = swap(field)
            re.append(jnp.where(low, field, other))
            im.append(jnp.where(low, -other, field))
            density.append((re[r] * resident - im[r] * swapped).astype(jnp.bfloat16))
        both = jnp.concatenate(density, axis=1)

        def fourier(fields, x_ref):
            for i in range(2):
                held[i * cells_yz : (i + 1) * cells_yz, :] = jnp.dot(
                    fields, x_ref[i], preferred_element_type=jnp.float32
                ).astype(jnp.bfloat16)
            return jnp.dot(w_ref[...], held[...], preferred_element_type=jnp.float32)

        spectrum = fourier(both, fwd_ref)
        screened = (spectrum * jnp.concatenate([kernel] * OCC_DEV, axis=1)).astype(jnp.bfloat16)
        potential = fourier(screened, inv_ref)
        for r in range(OCC_DEV):
            mine = potential[:, r * width : (r + 1) * width]
            term = re[r] * mine + im[r] * swap(mine)
            total = term if total is None else total + term
    out_ref[...] = (prefactor * total).astype(jnp.bfloat16)


def local(k_total, devices, targets, occupied, wavevectors, umklapp, owners):
    grid_y, grid_z, last_width = targets.shape[2:]
    grid_x = last_width // 2
    cells_yz = grid_y * grid_z
    vis = visitors(owners, occupied.reshape(OCC_DEV, cells_yz, last_width), k_total, devices)
    vmem = pl.BlockSpec(memory_space=pltpu.VMEM)
    smem = pl.BlockSpec(memory_space=pltpu.SMEM)
    out = pl.pallas_call(
        functools.partial(exchange_kernel, k_total, devices, (grid_y, grid_z, grid_x)),
        out_shape=jax.ShapeDtypeStruct((cells_yz, last_width), jnp.bfloat16),
        in_specs=[smem, smem, vmem, vmem, vmem, vmem, vmem],
        out_specs=vmem,
        scratch_shapes=[pltpu.VMEM((2 * cells_yz, OCC_DEV * last_width), jnp.bfloat16)],
        compiler_params=pltpu.CompilerParams(vmem_limit_bytes=32 * 1024 * 1024),
    )(
        wavevectors,
        umklapp,
        targets.reshape(cells_yz, last_width),
        vis,
        jnp.asarray(yz_matrix(grid_y, grid_z).astype(ml_dtypes.bfloat16)),
        jnp.asarray(x_matrices(grid_x, 1.0).astype(ml_dtypes.bfloat16)),
        jnp.asarray(x_matrices(grid_x, -1.0).astype(ml_dtypes.bfloat16)),
    )
    return out.reshape(targets.shape)


def solution(mesh):
    placed = (
        P("ka", "band", None, None, None),
        P("ka", "band", None, None, None),
        P(),
        P("ka", None, None),
        P("ka", None, None),
    )
    return jax.shard_map(
        functools.partial(local, mesh.shape["ka"], mesh.shape["band"]),
        mesh=mesh,
        in_specs=placed,
        out_specs=P("ka", "band", None, None, None),
        check_vma=False,
    )
```

```python
import functools
import math

import jax
import jax.numpy as jnp
import ml_dtypes
import numpy as np
from jax import lax
from jax.experimental import pallas as pl
from jax.experimental.pallas import tpu as pltpu
from jax.sharding import PartitionSpec as P

OCC_DEV = 2
STEPS = 2
KGRID = 4

screening_sq = 0.16
spacing = 0.25
prefactor = -0.5

MESH = pl.DeviceIdType.MESH
CORES = 2


def tables(length):
    indices = np.arange(length)
    angles = (indices[:, None] * indices[None, :] % length) * (2.0 * math.pi / length)

    def rounded(values):
        return values.astype(np.float32).astype(ml_dtypes.bfloat16).astype(np.float32)

    return rounded(np.cos(angles)), rounded(np.sin(angles))


def x_matrices(length, sign_value):
    cosine, sine = tables(length)
    upper = np.concatenate([cosine, -sign_value * sine], axis=1)
    lower = np.concatenate([sign_value * sine, cosine], axis=1)
    plain = np.concatenate([upper, lower], axis=0)
    turned = np.concatenate(
        [sign_value * plain[:, length:], -sign_value * plain[:, :length]], axis=1
    )
    two = np.eye(OCC_DEV, dtype=np.float32)
    return np.stack([np.kron(two, plain), np.kron(two, turned)])


def yz_matrix(grid_y, grid_z):
    cos_y, sin_y = tables(grid_y)
    cos_z, sin_z = tables(grid_z)
    cosine = np.kron(cos_y, cos_z) - np.kron(sin_y, sin_z)
    sine = np.kron(sin_y, cos_z) + np.kron(cos_y, sin_z)
    return np.concatenate([cosine, sine], axis=1)


def slices_of(cells_yz, devices):
    rows = -(-cells_yz // (devices * 16)) * 16
    return rows, -(-cells_yz // rows)


def exchange_kernel(k_total, devices, grid, owners_hbm, waves_hbm, umk_hbm, occ_hbm, t_hbm, w_hbm,
                    fwd_hbm, inv_hbm, out_ref, owners_ref, waves_ref, umk_ref, occ_ref, t_ref,
                    w_ref, fwd_ref, inv_ref, vis_ref, gath, stage, own_out, own_in, held, coul,
                    load, send1, recv1, send_own, recv_own, send2, recv2, send3, recv3):
    point = lax.axis_index("ka")
    me = lax.axis_index("band")
    level, core = lax.div(me, CORES), lax.rem(me, CORES)
    levels = devices // CORES
    grid_y, grid_z, grid_x = grid
    width = 2 * grid_x
    cells_yz = grid_y * grid_z
    cells = float(cells_yz * grid_x)
    rows, count = slices_of(cells_yz, devices)
    overlap = count * rows - cells_yz
    whole = cells_yz // rows * rows
    tail = cells_yz - whole

    loads = [
        pltpu.make_async_copy(source, target, load.at[i])
        for i, (source, target) in enumerate((
            (owners_hbm, owners_ref), (occ_hbm, occ_ref), (waves_hbm, waves_ref),
            (umk_hbm, umk_ref), (t_hbm, t_ref), (fwd_hbm, fwd_ref), (w_hbm, w_ref),
            (inv_hbm, inv_ref),
        ))
    ]
    for copy in loads:
        copy.start()

    def start_of(device):
        part = lax.rem(device, count)
        return pl.multiple_of(part * rows - lax.div(part, max(count - 1, 1)) * overlap, 16)

    def point_at(distance):
        return lax.rem(point + distance + k_total, k_total)

    def band_at(distance):
        return lax.rem(me + distance + devices, devices)

    def level_at(distance):
        return lax.rem(level + distance + levels, levels)

    barrier = pltpu.get_barrier_semaphore()
    greeted = [(point, band_at(-d)) for d in range(1, devices)]
    for s in range(1, STEPS + 1):
        greeted += [(point_at(-s), level_at(-d) * CORES + core) for d in range(levels)]
        greeted.append((point_at(s), me))
    for device in greeted:
        pl.semaphore_signal(barrier, inc=1, device_id=device, device_id_type=MESH)
    loads[0].wait()
    for s in range(STEPS):
        for r in range(OCC_DEV):
            own_out[s, r] = jnp.full((8, 128), owners_ref[0, s, r], jnp.int32).astype(jnp.float32)
    loads[1].wait()
    pl.semaphore_wait(barrier, len(greeted))

    owns = []
    for s in range(1, STEPS + 1):
        copy = pltpu.make_async_remote_copy(
            src_ref=own_out.at[s - 1], dst_ref=own_in.at[s - 1],
            send_sem=send_own.at[s - 1], recv_sem=recv_own.at[s - 1],
            device_id=(point_at(-s), me), device_id_type=MESH)
        copy.start()
        owns.append(copy)
    first = []
    for d in range(1, devices):
        target = band_at(d)
        copy = pltpu.make_async_remote_copy(
            src_ref=occ_ref.at[:, pl.ds(start_of(target), rows), :], dst_ref=gath.at[d],
            send_sem=send1.at[d], recv_sem=recv1.at[d],
            device_id=(point, target), device_id_type=MESH)
        copy.start()
        first.append(copy)
    gath[0] = occ_ref[:, pl.ds(start_of(me), rows), :]

    def swap(values):
        return pltpu.roll(values, grid_x, axis=1)

    def square(dim, length, shift):
        shape = (grid_y, grid_z, width)
        index = lax.broadcasted_iota(jnp.int32, shape, dim)
        if dim == 2:
            index = jnp.where(index < grid_x, index, index - grid_x)
        signed = jnp.where(index * 2 < length, index, index - length)
        wave = 2.0 * math.pi / (length * spacing) * (signed.astype(jnp.float32) + shift)
        return wave * wave

    for copy in loads[2:]:
        copy.wait()
    for s in range(STEPS):
        visit = point_at(-(s + 1))
        shift = [
            (waves_ref[point, a] - waves_ref[visit, a]).astype(jnp.float32) / KGRID
            + umk_ref[0, s, a].astype(jnp.float32)
            for a in range(3)
        ]
        squares = (
            square(0, grid_y, shift[1])
            + square(1, grid_z, shift[2])
            + square(2, grid_x, shift[0])
            + screening_sq
        )
        coul[s] = (4.0 * math.pi / cells / squares).reshape(cells_yz, width)

    for copy in owns + first:
        copy.wait_recv()

    def place(device):
        return pl.ds(pl.multiple_of(device * rows, 16), rows)

    second = [[] for _ in range(STEPS)]
    third = [[] for _ in range(STEPS)]
    for s in range(STEPS):
        for r in range(OCC_DEV):
            owner = own_in[s, r]
            chosen = jnp.zeros((rows // 8, 8, 128), jnp.float32)
            for d in range(devices):
                here = (owner == band_at(-d).astype(jnp.float32))[None]
                chosen = jnp.where(
                    here, gath[d, r].astype(jnp.float32).reshape(rows // 8, 8, 128), chosen
                )
            stage[s, r] = chosen.reshape(rows, 128).astype(jnp.bfloat16)
        for d in range(levels):
            copy = pltpu.make_async_remote_copy(
                src_ref=stage.at[s], dst_ref=vis_ref.at[s, :, place(me), :],
                send_sem=send2.at[s, d], recv_sem=recv2.at[s, d],
                device_id=(point_at(s + 1), level_at(d) * CORES + core), device_id_type=MESH)
            copy.start()
            second[s].append(copy)

    def pass_on(s):
        for d, copy in enumerate(second[s]):
            copy.wait_recv()
            arrived = vis_ref.at[s, :, place(level_at(-d) * CORES + core), :]
            across = pltpu.make_async_remote_copy(
                src_ref=arrived, dst_ref=arrived,
                send_sem=send3.at[s, d], recv_sem=recv3.at[s, d],
                device_id=(point, level * CORES + 1 - core), device_id_type=MESH)
            across.start()
            third[s].append(across)

    low = lax.broadcasted_iota(jnp.int32, (cells_yz, width), 1) < grid_x

    def fourier(fields, x_ref):
        for i in range(2):
            held[i * cells_yz : (i + 1) * cells_yz, :] = jnp.dot(
                fields, x_ref[i], preferred_element_type=jnp.float32
            ).astype(jnp.bfloat16)
        return jnp.dot(w_ref[...], held[...], preferred_element_type=jnp.float32)

    total = None
    for s in range(STEPS):
        pass_on(s)
        for copy in third[s]:
            copy.wait_recv()
        resident = t_ref[...].astype(jnp.float32)
        swapped = swap(resident)
        re, im, density = [], [], []
        for r in range(OCC_DEV):
            field = vis_ref[s, r, :whole]
            if tail:
                end = whole + rows
                field = jnp.concatenate([field, vis_ref[s, r, end - tail : end]], axis=0)
            field = field.astype(jnp.float32)
            other = swap(field)
            re.append(jnp.where(low, field, other))
            im.append(jnp.where(low, -other, field))
            density.append((re[r] * resident - im[r] * swapped).astype(jnp.bfloat16))
        spectrum = fourier(jnp.concatenate(density, axis=1), fwd_ref)
        kernel = coul[s]
        screened = (spectrum * jnp.concatenate([kernel] * OCC_DEV, axis=1)).astype(jnp.bfloat16)
        potential = fourier(screened, inv_ref)
        for r in range(OCC_DEV):
            mine = potential[:, r * width : (r + 1) * width]
            term = re[r] * mine + im[r] * swap(mine)
            total = term if total is None else total + term
    out_ref[...] = (prefactor * total).astype(jnp.bfloat16)
    for copy in owns + first + second[0] + second[1] + third[0] + third[1]:
        copy.wait_send()


def local(k_total, devices, targets, occupied, wavevectors, umklapp, owners):
    grid_y, grid_z, last_width = targets.shape[2:]
    grid_x = last_width // 2
    cells_yz = grid_y * grid_z
    rows, _ = slices_of(cells_yz, devices)
    levels = devices // CORES
    dma = pltpu.SemaphoreType.DMA
    hbm = pl.BlockSpec(memory_space=pltpu.HBM)
    args = (
        owners,
        wavevectors,
        umklapp,
        occupied.reshape(OCC_DEV, cells_yz, last_width),
        targets.reshape(cells_yz, last_width),
        jnp.asarray(yz_matrix(grid_y, grid_z).astype(ml_dtypes.bfloat16)),
        jnp.asarray(x_matrices(grid_x, 1.0).astype(ml_dtypes.bfloat16)),
        jnp.asarray(x_matrices(grid_x, -1.0).astype(ml_dtypes.bfloat16)),
    )
    out = pl.pallas_call(
        functools.partial(exchange_kernel, k_total, devices, (grid_y, grid_z, grid_x)),
        out_shape=jax.ShapeDtypeStruct((cells_yz, last_width), jnp.bfloat16),
        in_specs=[hbm] * len(args),
        out_specs=pl.BlockSpec(memory_space=pltpu.VMEM),
        scratch_shapes=[pltpu.SMEM(x.shape, x.dtype) for x in args[:3]]
        + [pltpu.VMEM(x.shape, x.dtype) for x in args[3:]]
        + [
            pltpu.VMEM((STEPS, OCC_DEV, devices * rows, 128), jnp.bfloat16),
            pltpu.VMEM((devices, OCC_DEV, rows, 128), jnp.bfloat16),
            pltpu.VMEM((STEPS, OCC_DEV, rows, 128), jnp.bfloat16),
            pltpu.VMEM((STEPS, OCC_DEV, 8, 128), jnp.float32),
            pltpu.VMEM((STEPS, OCC_DEV, 8, 128), jnp.float32),
            pltpu.VMEM((2 * cells_yz, OCC_DEV * last_width), jnp.bfloat16),
            pltpu.VMEM((STEPS, cells_yz, last_width), jnp.float32),
            dma((len(args),)),
            dma((devices,)), dma((devices,)), dma((STEPS,)), dma((STEPS,)),
            dma((STEPS, levels)), dma((STEPS, levels)),
            dma((STEPS, levels)), dma((STEPS, levels)),
        ],
        compiler_params=pltpu.CompilerParams(
            collective_id=0, has_side_effects=True, vmem_limit_bytes=62 * 1024 * 1024
        ),
    )(*args)
    return out.reshape(targets.shape)


def solution(mesh):
    placed = (
        P("ka", "band", None, None, None),
        P("ka", "band", None, None, None),
        P(),
        P("ka", None, None),
        P("ka", None, None),
    )
    return jax.shard_map(
        functools.partial(local, mesh.shape["ka"], mesh.shape["band"]),
        mesh=mesh,
        in_specs=placed,
        out_specs=P("ka", "band", None, None, None),
        check_vma=False,
    )
```

```python
import functools
import math

import jax
import jax.numpy as jnp
import ml_dtypes
import numpy as np
from jax import lax
from jax.experimental import pallas as pl
from jax.experimental.pallas import tpu as pltpu
from jax.sharding import PartitionSpec as P

OCC_DEV = 2
STEPS = 2
KGRID = 4

screening_sq = 0.16
spacing = 0.25
prefactor = -0.5

MESH = pl.DeviceIdType.MESH
CORES = 2


def tables(length):
    indices = np.arange(length)
    angles = (indices[:, None] * indices[None, :] % length) * (2.0 * math.pi / length)

    def rounded(values):
        return values.astype(np.float32).astype(ml_dtypes.bfloat16).astype(np.float32)

    return rounded(np.cos(angles)), rounded(np.sin(angles))


def x_matrices(length, sign_value):
    cosine, sine = tables(length)
    upper = np.concatenate([cosine, -sign_value * sine], axis=1)
    lower = np.concatenate([sign_value * sine, cosine], axis=1)
    plain = np.concatenate([upper, lower], axis=0)
    turned = np.concatenate(
        [sign_value * plain[:, length:], -sign_value * plain[:, :length]], axis=1
    )
    two = np.eye(STEPS, dtype=np.float32)
    return np.stack([np.kron(two, plain), np.kron(two, turned)])


def yz_matrix(grid_y, grid_z):
    cos_y, sin_y = tables(grid_y)
    cos_z, sin_z = tables(grid_z)
    cosine = np.kron(cos_y, cos_z) - np.kron(sin_y, sin_z)
    sine = np.kron(sin_y, cos_z) + np.kron(cos_y, sin_z)
    return np.concatenate([cosine, sine], axis=1)


def slices_of(cells_yz, devices):
    rows = -(-cells_yz // (devices * 16)) * 16
    return rows, -(-cells_yz // rows)


def exchange_kernel(k_total, devices, grid, owners_hbm, waves_hbm, umk_hbm, occ_hbm, t_hbm, w_hbm,
                    fwd_hbm, inv_hbm, out_ref, owners_ref, waves_ref, umk_ref, occ_ref, t_ref,
                    w_ref, fwd_ref, inv_ref, vis_ref, gath, stage, own_out, own_in, held, coul,
                    load, send1, recv1, send_own, recv_own, send2, recv2, send3, recv3):
    point = lax.axis_index("ka")
    me = lax.axis_index("band")
    level, core = lax.div(me, CORES), lax.rem(me, CORES)
    levels = devices // CORES
    grid_y, grid_z, grid_x = grid
    width = 2 * grid_x
    cells_yz = grid_y * grid_z
    cells = float(cells_yz * grid_x)
    rows, count = slices_of(cells_yz, devices)
    overlap = count * rows - cells_yz
    whole = cells_yz // rows * rows
    tail = cells_yz - whole

    loads = [
        pltpu.make_async_copy(source, target, load.at[i])
        for i, (source, target) in enumerate((
            (owners_hbm, owners_ref), (occ_hbm, occ_ref), (waves_hbm, waves_ref),
            (umk_hbm, umk_ref), (t_hbm, t_ref), (fwd_hbm, fwd_ref), (w_hbm, w_ref),
            (inv_hbm, inv_ref),
        ))
    ]
    for copy in loads:
        copy.start()

    def start_of(device):
        part = lax.rem(device, count)
        return pl.multiple_of(part * rows - lax.div(part, max(count - 1, 1)) * overlap, 16)

    def point_at(distance):
        return lax.rem(point + distance + k_total, k_total)

    def band_at(distance):
        return lax.rem(me + distance + devices, devices)

    def level_at(distance):
        return lax.rem(level + distance + levels, levels)

    barrier = pltpu.get_barrier_semaphore()
    greeted = [(point, band_at(-d)) for d in range(1, devices)]
    for s in range(1, STEPS + 1):
        greeted += [(point_at(-s), level_at(-d) * CORES + core) for d in range(levels)]
        greeted.append((point_at(s), me))
    for device in greeted:
        pl.semaphore_signal(barrier, inc=1, device_id=device, device_id_type=MESH)
    loads[0].wait()
    for s in range(STEPS):
        for r in range(OCC_DEV):
            own_out[s, r] = jnp.full((8, 128), owners_ref[0, s, r], jnp.int32).astype(jnp.float32)
    loads[1].wait()
    pl.semaphore_wait(barrier, len(greeted))

    owns = []
    for s in range(1, STEPS + 1):
        copy = pltpu.make_async_remote_copy(
            src_ref=own_out.at[s - 1], dst_ref=own_in.at[s - 1],
            send_sem=send_own.at[s - 1], recv_sem=recv_own.at[s - 1],
            device_id=(point_at(-s), me), device_id_type=MESH)
        copy.start()
        owns.append(copy)
    first = [[] for _ in range(OCC_DEV)]
    for r in range(OCC_DEV):
        for d in range(1, devices):
            target = band_at(d)
            copy = pltpu.make_async_remote_copy(
                src_ref=occ_ref.at[r, pl.ds(start_of(target), rows), :], dst_ref=gath.at[d, r],
                send_sem=send1.at[r, d], recv_sem=recv1.at[r, d],
                device_id=(point, target), device_id_type=MESH)
            copy.start()
            first[r].append(copy)
    gath[0] = occ_ref[:, pl.ds(start_of(me), rows), :]

    def swap(values):
        return pltpu.roll(values, grid_x, axis=1)

    def square(dim, length, shift):
        shape = (grid_y, grid_z, width)
        index = lax.broadcasted_iota(jnp.int32, shape, dim)
        if dim == 2:
            index = jnp.where(index < grid_x, index, index - grid_x)
        signed = jnp.where(index * 2 < length, index, index - length)
        wave = 2.0 * math.pi / (length * spacing) * (signed.astype(jnp.float32) + shift)
        return wave * wave

    for copy in loads[2:]:
        copy.wait()
    for s in range(STEPS):
        visit = point_at(-(s + 1))
        shift = [
            (waves_ref[point, a] - waves_ref[visit, a]).astype(jnp.float32) / KGRID
            + umk_ref[0, s, a].astype(jnp.float32)
            for a in range(3)
        ]
        squares = (
            square(0, grid_y, shift[1])
            + square(1, grid_z, shift[2])
            + square(2, grid_x, shift[0])
            + screening_sq
        )
        coul[s] = (4.0 * math.pi / cells / squares).reshape(cells_yz, width)

    def place(device):
        return pl.ds(pl.multiple_of(device * rows, 16), rows)

    second = [[] for _ in range(OCC_DEV)]
    third = [[] for _ in range(OCC_DEV)]
    for r in range(OCC_DEV):
        for copy in (owns if r == 0 else []) + first[r]:
            copy.wait_recv()
        for s in range(STEPS):
            owner = own_in[s, r]
            chosen = jnp.zeros((rows // 8, 8, 128), jnp.float32)
            for d in range(devices):
                here = (owner == band_at(-d).astype(jnp.float32))[None]
                chosen = jnp.where(
                    here, gath[d, r].astype(jnp.float32).reshape(rows // 8, 8, 128), chosen
                )
            stage[s, r] = chosen.reshape(rows, 128).astype(jnp.bfloat16)
            for d in range(levels):
                copy = pltpu.make_async_remote_copy(
                    src_ref=stage.at[s, r], dst_ref=vis_ref.at[s, r, place(me), :],
                    send_sem=send2.at[r, s, d], recv_sem=recv2.at[r, s, d],
                    device_id=(point_at(s + 1), level_at(d) * CORES + core), device_id_type=MESH)
                copy.start()
                second[r].append((s, d, copy))

    def pass_on(r):
        for s, d, copy in second[r]:
            copy.wait_recv()
            arrived = vis_ref.at[s, r, place(level_at(-d) * CORES + core), :]
            across = pltpu.make_async_remote_copy(
                src_ref=arrived, dst_ref=arrived,
                send_sem=send3.at[r, s, d], recv_sem=recv3.at[r, s, d],
                device_id=(point, level * CORES + 1 - core), device_id_type=MESH)
            across.start()
            third[r].append(across)

    low = lax.broadcasted_iota(jnp.int32, (cells_yz, width), 1) < grid_x

    def fourier(fields, x_ref):
        for i in range(2):
            held[i * cells_yz : (i + 1) * cells_yz, :] = jnp.dot(
                fields, x_ref[i], preferred_element_type=jnp.float32
            ).astype(jnp.bfloat16)
        return jnp.dot(w_ref[...], held[...], preferred_element_type=jnp.float32)

    total = None
    kernel = jnp.concatenate([coul[s] for s in range(STEPS)], axis=1)
    for r in range(OCC_DEV):
        pass_on(r)
        for copy in third[r]:
            copy.wait_recv()
        resident = t_ref[...].astype(jnp.float32)
        swapped = swap(resident)
        re, im, density = [], [], []
        for s in range(STEPS):
            field = vis_ref[s, r, :whole]
            if tail:
                end = whole + rows
                field = jnp.concatenate([field, vis_ref[s, r, end - tail : end]], axis=0)
            field = field.astype(jnp.float32)
            other = swap(field)
            re.append(jnp.where(low, field, other))
            im.append(jnp.where(low, -other, field))
            density.append((re[s] * resident - im[s] * swapped).astype(jnp.bfloat16))
        spectrum = fourier(jnp.concatenate(density, axis=1), fwd_ref)
        potential = fourier((spectrum * kernel).astype(jnp.bfloat16), inv_ref)
        for s in range(STEPS):
            mine = potential[:, s * width : (s + 1) * width]
            term = re[s] * mine + im[s] * swap(mine)
            total = term if total is None else total + term
    out_ref[...] = (prefactor * total).astype(jnp.bfloat16)
    for copy in owns:
        copy.wait_send()
    for r in range(OCC_DEV):
        for copy in first[r] + [entry[-1] for entry in second[r]] + third[r]:
            copy.wait_send()


def local(k_total, devices, targets, occupied, wavevectors, umklapp, owners):
    grid_y, grid_z, last_width = targets.shape[2:]
    grid_x = last_width // 2
    cells_yz = grid_y * grid_z
    rows, _ = slices_of(cells_yz, devices)
    levels = devices // CORES
    dma = pltpu.SemaphoreType.DMA
    hbm = pl.BlockSpec(memory_space=pltpu.HBM)
    args = (
        owners,
        wavevectors,
        umklapp,
        occupied.reshape(OCC_DEV, cells_yz, last_width),
        targets.reshape(cells_yz, last_width),
        jnp.asarray(yz_matrix(grid_y, grid_z).astype(ml_dtypes.bfloat16)),
        jnp.asarray(x_matrices(grid_x, 1.0).astype(ml_dtypes.bfloat16)),
        jnp.asarray(x_matrices(grid_x, -1.0).astype(ml_dtypes.bfloat16)),
    )
    out = pl.pallas_call(
        functools.partial(exchange_kernel, k_total, devices, (grid_y, grid_z, grid_x)),
        out_shape=jax.ShapeDtypeStruct((cells_yz, last_width), jnp.bfloat16),
        in_specs=[hbm] * len(args),
        out_specs=pl.BlockSpec(memory_space=pltpu.VMEM),
        scratch_shapes=[pltpu.SMEM(x.shape, x.dtype) for x in args[:3]]
        + [pltpu.VMEM(x.shape, x.dtype) for x in args[3:]]
        + [
            pltpu.VMEM((STEPS, OCC_DEV, devices * rows, 128), jnp.bfloat16),
            pltpu.VMEM((devices, OCC_DEV, rows, 128), jnp.bfloat16),
            pltpu.VMEM((STEPS, OCC_DEV, rows, 128), jnp.bfloat16),
            pltpu.VMEM((STEPS, OCC_DEV, 8, 128), jnp.float32),
            pltpu.VMEM((STEPS, OCC_DEV, 8, 128), jnp.float32),
            pltpu.VMEM((2 * cells_yz, STEPS * last_width), jnp.bfloat16),
            pltpu.VMEM((STEPS, cells_yz, last_width), jnp.float32),
            dma((len(args),)),
            dma((OCC_DEV, devices)), dma((OCC_DEV, devices)), dma((STEPS,)), dma((STEPS,)),
            dma((OCC_DEV, STEPS, levels)), dma((OCC_DEV, STEPS, levels)),
            dma((OCC_DEV, STEPS, levels)), dma((OCC_DEV, STEPS, levels)),
        ],
        compiler_params=pltpu.CompilerParams(
            collective_id=0, has_side_effects=True, vmem_limit_bytes=62 * 1024 * 1024
        ),
    )(*args)
    return out.reshape(targets.shape)


def solution(mesh):
    placed = (
        P("ka", "band", None, None, None),
        P("ka", "band", None, None, None),
        P(),
        P("ka", None, None),
        P("ka", None, None),
    )
    return jax.shard_map(
        functools.partial(local, mesh.shape["ka"], mesh.shape["band"]),
        mesh=mesh,
        in_specs=placed,
        out_specs=P("ka", "band", None, None, None),
        check_vma=False,
    )
```
